512 devices in a mesh: ctx: 64 (over z, x), tp: 8 (over y, core).
Axes of the slice: x: 4, y: 4, z: 16, core: 2. Of those that a mesh axis runs over, the one named last changes fastest.
Arguments:
- queries: bfloat16 [16384, 16384], P('ctx', 'tp'), may hold values from -4 to 4
- keys: bfloat16 [16384, 1024], P('ctx', 'tp'), may hold values from -4 to 4
- values: bfloat16 [16384, 1024], P('ctx', 'tp'), may hold values from -4 to 4
- attn_out: bfloat16 [16384, 16384], P('ctx', 'tp'), may hold values from -4 to 4
- grad_out: bfloat16 [16384, 16384], P('ctx', 'tp'), may hold values from -8 to 8
- log_norm: float32 [128, 16384], P('tp', 'ctx'), may hold values from 0 to 4
- doc_start: int32 [16384], P('ctx'), may hold values from 0 to 16383, as said below
Outputs:
- grad_queries: bfloat16 [16384, 16384], P('ctx', 'tp')
- grad_keys: bfloat16 [16384, 1024], P('ctx', 'tp')
- grad_values: bfloat16 [16384, 1024], P('ctx', 'tp')
- grad_square_mean: float32 [], replicated
The draws below stay inside these ranges and needn't reach their ends.
Inputs may be any that keep to these rules, and one draw needn't show every extreme that they name: doc_start is non-decreasing, doc_start[p] <= p and p - doc_start[p] < 1024; a document is the run of tokens with equal doc_start, beginning at that position; at least one document holds exactly 1024 tokens; the last token forms a document of its own.
All inputs are finite; a program needn't handle non-finite values.
Results may differ from the reference program's by a relative error of at most 0.0086.
Values may be sent and summed in bfloat16 or wider, within the bound.
No kernel may reach another device: no remote copies, remote signals or barrier semaphores. Data moves between devices by JAX's collectives and lax.ppermute only.
A program may use at most 64 MiB of HBM per device.

```python
import math
import jax
import jax.numpy as jnp
from jax import lax

HEADS = 128
KV = 8
HD = 128
S_DEV = 256
REACH = 4
DOC_MAX = 1024
TOKENS = 16384
N_CTX = 64


def draw_doc_start(key, part):
    key = jax.random.fold_in(key, 11)
    first_key, second_key, third_key, fourth_key = jax.random.split(key, 4)
    long_lengths = jax.random.randint(first_key, (TOKENS,), 1, DOC_MAX + 1)
    short_lengths = jax.random.randint(second_key, (TOKENS,), 1, DOC_MAX // 8 + 1)
    coin = jax.random.randint(third_key, (TOKENS,), 0, 2)
    lengths = jnp.where(coin == 1, long_lengths, short_lengths).astype(jnp.int32)
    picked = jax.random.randint(fourth_key, (), 0, 3)
    lengths = jnp.where(jnp.arange(TOKENS, dtype=jnp.int32) == picked, DOC_MAX, lengths).astype(jnp.int32)
    ends = jnp.cumsum(lengths).astype(jnp.int32)
    positions = jnp.arange(TOKENS, dtype=jnp.int32)
    index = jnp.searchsorted(ends, positions, side='right').astype(jnp.int32)
    starts = jnp.concatenate([jnp.zeros((1,), jnp.int32), ends[:-1]])
    result = starts[index].astype(jnp.int32)
    return jnp.where(positions == TOKENS - 1, TOKENS - 1, result).astype(jnp.int32)


def draw_grad_out(key, part):
    key = jax.random.fold_in(key, 23)
    base_key, row_key, head_key = jax.random.split(key, 3)
    shape = (TOKENS, HEADS * HD)
    base = jax.random.truncated_normal(base_key, -4.0, 4.0, shape, jnp.float32)
    row_scale = jnp.exp(jax.random.uniform(row_key, (TOKENS, 1), jnp.float32) * math.log(10.0))
    head_scale = jnp.exp(jax.random.uniform(head_key, (1, HEADS), jnp.float32) * math.log(10.0))
    row_ramp = 1.0 + 2.0 * jnp.arange(TOKENS, dtype=jnp.float32)[:, None] / (TOKENS - 1)
    head_ramp = 1.0 + 2.0 * jnp.arange(HEADS, dtype=jnp.float32)[None, :] / (HEADS - 1)
    columns = jnp.repeat(head_scale * head_ramp, HD, axis=1)
    return (0.002 * base * row_scale * row_ramp * columns).astype(jnp.bfloat16)


def block_levels(stream_key, extent, shards, least, largest):
    def one(dim, blocks):
        steps = jax.random.uniform(jax.random.fold_in(jax.random.fold_in(stream_key, 6), dim), (blocks,), jnp.float32, least / len(shards), largest / len(shards))
        return jnp.repeat(jnp.exp(steps), extent[dim] // blocks).reshape((-1,) + (1,) * (len(extent) - dim - 1))

    factor_of = one(*shards[0])
    for cut in shards[1:]:
        factor_of = factor_of * one(*cut)
    return factor_of


def bell_draw(key, shape, deviation, bound, cuts=(), kind=jnp.bfloat16):
    entries = deviation * jax.random.normal(key, shape, jnp.float32)
    if cuts:
        entries = entries * block_levels(key, shape, cuts, -0.22, 0.18)
    return jnp.clip(entries, -bound, bound).astype(kind)


def setup_inputs(seed: int = 0) -> dict:
    splits = jax.random.split(jax.random.key(seed), 8)
    return {
        "queries": bell_draw(splits[0], (TOKENS, HEADS * HD), 1.0, 4.0, ((0, 64), (1, 8))),
        "keys": bell_draw(splits[1], (TOKENS, KV * HD), 1.0, 4.0, ((0, 64), (1, 8))),
        "values": bell_draw(splits[2], (TOKENS, KV * HD), 1.0, 4.0, ((0, 64), (1, 8))),
        "attn_out": bell_draw(splits[3], (TOKENS, HEADS * HD), 1.0, 4.0, ((0, 64), (1, 8))),
        "grad_out": draw_grad_out(jax.random.fold_in(splits[7], 71), 0),
        "log_norm": jnp.clip(4.0 * jax.random.uniform(splits[5], (HEADS, TOKENS), jnp.float32) ** block_levels(splits[5], (HEADS, TOKENS), ((0, 8), (1, 64)), -0.2, 0.2), 0.0, 4.0),
        "doc_start": draw_doc_start(jax.random.fold_in(splits[7], 71), 0),
    }


def reference(queries, keys, values, attn_out, grad_out, log_norm, doc_start):
    scale = HD ** -0.5
    group = HEADS // KV
    margin = REACH * S_DEV
    window = margin + S_DEV
    query_heads = queries.reshape(TOKENS, KV, group, HD)
    grad_heads = grad_out.reshape(TOKENS, KV, group, HD)
    out_heads = attn_out.reshape(TOKENS, KV, group, HD)
    delta = jnp.sum(grad_heads.astype(jnp.float32) * out_heads.astype(jnp.float32), axis=-1)
    norms = log_norm.reshape(KV, group, TOKENS)
    pad_keys = jnp.concatenate([jnp.zeros((margin, KV, HD), jnp.bfloat16), keys.reshape(TOKENS, KV, HD)], axis=0)
    pad_values = jnp.concatenate([jnp.zeros((margin, KV, HD), jnp.bfloat16), values.reshape(TOKENS, KV, HD)], axis=0)

    def step(carry, tile):
        first = (tile * S_DEV).astype(jnp.int32)
        query_tile = lax.dynamic_slice_in_dim(query_heads, first, S_DEV, 0).astype(jnp.float32)
        grad_tile = lax.dynamic_slice_in_dim(grad_heads, first, S_DEV, 0).astype(jnp.float32)
        delta_tile = jnp.transpose(lax.dynamic_slice_in_dim(delta, first, S_DEV, 0), (1, 2, 0))
        norm_tile = lax.dynamic_slice_in_dim(norms, first, S_DEV, 2)
        start_tile = lax.dynamic_slice_in_dim(doc_start, first, S_DEV, 0)
        key_tile = lax.dynamic_slice_in_dim(pad_keys, first, window, 0).astype(jnp.float32)
        value_tile = lax.dynamic_slice_in_dim(pad_values, first, window, 0).astype(jnp.float32)
        query_pos = first + jnp.arange(S_DEV, dtype=jnp.int32)
        key_pos = first - margin + jnp.arange(window, dtype=jnp.int32)
        allowed = (key_pos[None, :] >= start_tile[:, None]) & (key_pos[None, :] <= query_pos[:, None])
        scores = jnp.einsum("ikgd,jkd->kgij", query_tile, key_tile) * scale
        probs = jnp.where(allowed, jnp.exp(scores - norm_tile[..., None]), 0.0)
        dprobs = jnp.einsum("ikgd,jkd->kgij", grad_tile, value_tile)
        dscores = probs * (dprobs - delta_tile[..., None])
        probs_low = lax.optimization_barrier(probs.astype(jnp.bfloat16)).astype(jnp.float32)
        dscores_low = lax.optimization_barrier(dscores.astype(jnp.bfloat16)).astype(jnp.float32)
        grad_v = jnp.einsum("kgij,ikgd->jkd", probs_low, grad_tile)
        grad_k = jnp.einsum("kgij,ikgd->jkd", dscores_low, query_tile) * scale
        grad_q = jnp.einsum("kgij,jkd->ikgd", dscores_low, key_tile) * scale
        current = lax.dynamic_slice_in_dim(carry, first, window, 1)
        carry = lax.dynamic_update_slice_in_dim(carry, current + jnp.stack([grad_k, grad_v]), first, 1)
        return carry, grad_q

    start_carry = jnp.zeros((2, TOKENS + margin, KV, HD), jnp.float32)
    carry, grad_q = lax.scan(step, start_carry, jnp.arange(N_CTX, dtype=jnp.int32))
    grad_q = grad_q.reshape(TOKENS, HEADS * HD)
    grad_square_mean = jnp.mean(grad_q * grad_q)
    grad_keys = carry[0, margin:].reshape(TOKENS, KV * HD).astype(jnp.bfloat16)
    grad_values = carry[1, margin:].reshape(TOKENS, KV * HD).astype(jnp.bfloat16)
    return (grad_q.astype(jnp.bfloat16), grad_keys, grad_values, grad_square_mean)
```

```python
import functools
import math

import jax
import jax.numpy as jnp
from jax import lax
from jax.experimental import pallas as pl
from jax.experimental.pallas import tpu as pltpu
from jax.sharding import PartitionSpec as P

HD = 128
ROWS = 256
HEADS = 16
REACH = 4
ROW_X = 4
LOG2E = math.log2(math.e)
SCALE = HD**-0.5
NT = (((1,), (1,)), ((), ()))
NN = (((1,), (0,)), ((), ()))
BF16 = jnp.bfloat16
F32 = jnp.float32


def dot(a, b, dims=NN):
    return lax.dot_general(a, b, dims, preferred_element_type=F32)


def columns(h):
    return slice(h * HD, (h + 1) * HD)


def rows_of(h):
    return slice(h * ROWS, (h + 1) * ROWS)


def pieces(x):
    first = x.astype(BF16).astype(F32)
    rest = x - first
    second = rest.astype(BF16).astype(F32)
    return first, second, (rest - second).astype(BF16).astype(F32)


def prepare_kernel(q, g, o, norm, q_t, g_t, ext, ext_t):
    ones = jnp.ones((8, HD), BF16)
    place = lax.broadcasted_iota(jnp.int32, (8, ROWS), 0)
    for h in range(HEADS):
        q_t[:, rows_of(h)] = q[:, columns(h)].T
        g_t[:, rows_of(h)] = g[:, columns(h)].T
        product = g[:, columns(h)].astype(F32) * o[:, columns(h)].astype(F32)
        high = product.astype(BF16)
        low = (product - high.astype(F32)).astype(BF16)
        delta = dot(ones, high, NT) + dot(ones, low, NT)
        shift = jnp.broadcast_to(norm[h : h + 1, :] * (-(HD**0.5)), (8, ROWS))
        block = jnp.zeros((8, ROWS), F32)
        for r, term in enumerate(pieces(shift) + pieces(-delta)):
            block = jnp.where(place == r, term, block)
        ext_t[8 * h : 8 * h + 8, :] = block
    ext[...] = ext_t[...].T.astype(BF16)


def tile_grads(q, g, q_t, g_t, ext, k, v, bias, dq, dkv):
    lane = lax.broadcasted_iota(jnp.int32, (ROWS, HD), 1)
    k_wide = jnp.concatenate([k, jnp.where(lane % 8 < 3, 1.0, 0.0).astype(BF16)], axis=1)
    v_wide = jnp.concatenate([v, jnp.where((lane % 8 >= 3) & (lane % 8 < 6), 1.0, 0.0).astype(BF16)], axis=1)
    extras = [jnp.where(lane // 8 == h, ext[...], jnp.zeros((), BF16)) for h in range(HEADS)]
    q_wide = jnp.concatenate([jnp.concatenate([q[:, columns(h)], extras[h]], axis=1) for h in range(HEADS)], axis=0)
    g_wide = jnp.concatenate([jnp.concatenate([g[:, columns(h)], extras[h]], axis=1) for h in range(HEADS)], axis=0)
    scores = dot(q_wide, k_wide, NT)
    dprobs = dot(g_wide, v_wide, NT)
    probs = jnp.exp2(scores * (SCALE * LOG2E) + jnp.concatenate([bias[...]] * HEADS, axis=0))
    dscores = (probs * dprobs).astype(BF16)
    dq[...] += dot(dscores, k)
    dkv[:, :ROWS] = dot(q_t[...], dscores) * SCALE
    dkv[:, ROWS:] = dot(g_t[...], probs.astype(BF16))


def set_bias(bias, doc, ctx, offset):
    key_pos = (ctx - offset) * ROWS + lax.broadcasted_iota(jnp.int32, (ROWS, ROWS), 1)
    query_pos = ctx * ROWS + lax.broadcasted_iota(jnp.int32, (ROWS, ROWS), 0)
    bias[...] = jnp.where((key_pos >= doc[...]) & (key_pos <= query_pos), 0.0, -1e30)


def near_kernel(meta, doc, q, g, q_t, g_t, ext, own, far, dq, own_grads, far_grads, bias, dkv):
    ctx, first = meta[0], meta[1]
    dq[...] = jnp.zeros_like(dq)
    far_grads[...] = jnp.zeros_like(far_grads)
    set_bias(bias, doc, ctx, 0)
    tile_grads(q, g, q_t, g_t, ext, own[:ROWS], own[ROWS:], bias, dq, dkv)
    own_grads[:ROWS] = dkv[:, :ROWS].T
    own_grads[ROWS:] = dkv[:, ROWS:].T

    @pl.when(first < (ctx - REACH + 1) * ROWS)
    def _():
        set_bias(bias, doc, ctx, REACH)
        tile_grads(q, g, q_t, g_t, ext, far[:ROWS], far[ROWS:], bias, dq, dkv)
        far_grads[:ROWS] = dkv[:, :ROWS].T.astype(BF16)
        far_grads[ROWS:] = dkv[:, ROWS:].T.astype(BF16)


def between_kernel(meta, doc, q, g, q_t, g_t, ext, blocks, dq_in, far_grads, dq, squares, parts, total, bias, dkv):
    ctx, first = meta[0], meta[1]
    x = lax.rem(ctx, ROW_X)
    total[...] = dq_in[...]
    parts[...] = jnp.zeros_like(parts)
    parts[x] = far_grads[...]
    reach = jnp.clip(lax.div(ctx * ROWS - first + (ROWS - 1), ROWS), 0, REACH - 1)

    def one(offset, carry):
        slot = lax.rem(x - offset + ROW_X, ROW_X)
        set_bias(bias, doc, ctx, offset)
        tile_grads(q, g, q_t, g_t, ext, blocks[slot, :ROWS], blocks[slot, ROWS:], bias, total, dkv)
        parts[slot, :ROWS] = dkv[:, :ROWS].T.astype(BF16)
        parts[slot, ROWS:] = dkv[:, ROWS:].T.astype(BF16)
        return carry

    lax.fori_loop(1, reach + 1, one, 0)
    square = jnp.zeros((8, HD), F32)
    for h in range(HEADS):
        block = total[rows_of(h), :] * SCALE
        dq[:, columns(h)] = block.astype(BF16)
        square += jnp.sum((block * block).reshape(ROWS // 8, 8, HD), axis=0)
    squares[...] = jnp.broadcast_to(jnp.sum(square, axis=0, keepdims=True), (8, HD))


VMEM = pl.BlockSpec(memory_space=pltpu.VMEM)
SMEM = pl.BlockSpec(memory_space=pltpu.SMEM)


def call(kernel, outs, scratch, args, smem=0, limit=24, tiles=0.0):
    return pl.pallas_call(
        kernel,
        out_shape=tuple(jax.ShapeDtypeStruct(shape, dtype) for shape, dtype in outs),
        in_specs=[SMEM] * smem + [VMEM] * (len(args) - smem),
        out_specs=(VMEM,) * len(outs),
        scratch_shapes=[pltpu.VMEM(shape, dtype) for shape, dtype in scratch],
        compiler_params=pltpu.CompilerParams(vmem_limit_bytes=limit * 2**20),
        cost_estimate=pl.CostEstimate(
            flops=int(tiles * 10 * HEADS * ROWS * ROWS * HD), bytes_accessed=4 * 2**20, transcendentals=0
        ),
    )(*args)


def exchange_x(x):
    groups = [[z * ROW_X + i for i in range(ROW_X)] for z in range(lax.axis_size("ctx") // ROW_X)]
    return lax.all_to_all(x, "ctx", 0, 0, axis_index_groups=groups, tiled=True)


def shift_z(x, by):
    peers = lax.axis_size("ctx")
    return lax.ppermute(x, "ctx", [(i, (i + ROW_X * by) % peers) for i in range(peers)])


def shards(queries, keys, values, attn_out, grad_out, log_norm, doc_start):
    ctx = lax.axis_index("ctx")
    x = lax.rem(ctx, ROW_X)
    wide = ROWS * HEADS
    slots = jnp.arange(ROW_X, dtype=jnp.int32)[:, None, None]

    own = jnp.concatenate([keys, values], axis=0)
    far = shift_z(own, 1)
    meta = jnp.stack([ctx, doc_start[0]])
    doc = doc_start.reshape(ROWS, 1)
    q_t, g_t, ext = call(
        prepare_kernel,
        [((HD, wide), BF16), ((HD, wide), BF16), ((ROWS, HD), BF16)],
        [((HD, ROWS), F32)],
        (queries, grad_out, attn_out, log_norm),
        tiles=1.0,
    )
    far, q_t, g_t, ext = lax.optimization_barrier((far, q_t, g_t, ext))
    blocks = exchange_x(jnp.where(slots > x, own[None], far[None]))
    common = (meta, doc, queries, grad_out, q_t, g_t, ext)
    tile_scratch = [((ROWS, ROWS), F32), ((HD, 2 * ROWS), F32)]
    dq_near, own_grads, far_grads = call(
        near_kernel,
        [((wide, HD), F32), ((2 * ROWS, HD), F32), ((2 * ROWS, HD), BF16)],
        tile_scratch,
        common + (own, far),
        smem=1,
        tiles=2.0,
    )
    blocks, dq_near, own_grads, far_grads = lax.optimization_barrier((blocks, dq_near, own_grads, far_grads))
    grad_queries, squares, parts = call(
        between_kernel,
        [((ROWS, HEADS * HD), BF16), ((8, HD), F32), ((ROW_X, 2 * ROWS, HD), BF16)],
        [((wide, HD), F32)] + tile_scratch,
        common + (blocks, dq_near, far_grads),
        smem=1,
        tiles=3.0,
    )

    squares_tp = lax.all_to_all(squares, "tp", 0, 0, tiled=True)
    back = exchange_x(parts)
    peers = lax.axis_size("ctx")
    row = jnp.sum(squares_tp, axis=0, keepdims=True)
    squares_ctx = lax.all_to_all(jnp.broadcast_to(row, (peers, HD)), "ctx", 0, 0, tiled=True)
    back = back.astype(F32)
    onward = jnp.sum(jnp.where(slots <= x, back, 0.0), axis=0).astype(BF16)
    mine = jnp.sum(jnp.where(slots > x, back, 0.0), axis=0)
    grads = own_grads + mine + shift_z(onward, -1).astype(F32)
    entries = float(ROWS * peers * HEADS * lax.axis_size("tp") * HD)
    grad_square_mean = jnp.sum(squares_ctx) / entries
    grads = grads.astype(BF16)
    return (grad_queries, grads[:ROWS], grads[ROWS:], grad_square_mean)


def solution(mesh):
    return jax.shard_map(
        shards,
        mesh=mesh,
        in_specs=(
            P("ctx", "tp"),
            P("ctx", "tp"),
            P("ctx", "tp"),
            P("ctx", "tp"),
            P("ctx", "tp"),
            P("tp", "ctx"),
            P("ctx"),
        ),
        out_specs=(P("ctx", "tp"), P("ctx", "tp"), P("ctx", "tp"), P()),
        check_vma=False,
    )
```

```python
import functools
import math

import jax
import jax.numpy as jnp
from jax import lax
from jax.experimental import pallas as pl
from jax.experimental.pallas import tpu as pltpu
from jax.sharding import Mesh
from jax.sharding import PartitionSpec as P

HD = 128
ROWS = 256
HEADS = 16
REACH = 4
ROW_X = 4
LOG2E = math.log2(math.e)
SCALE = HD**-0.5
NT = (((1,), (1,)), ((), ()))
NN = (((1,), (0,)), ((), ()))
TN = (((0,), (0,)), ((), ()))
CHUNKS = 4
TAIL = 16
BF16 = jnp.bfloat16
F32 = jnp.float32


def dot(a, b, dims=NN):
    return lax.dot_general(a, b, dims, preferred_element_type=F32)


def columns(h):
    return slice(h * HD, (h + 1) * HD)


def rows_of(h):
    return slice(h * ROWS, (h + 1) * ROWS)


def pieces(x):
    first = x.astype(BF16).astype(F32)
    rest = x - first
    second = rest.astype(BF16).astype(F32)
    return first, second, (rest - second).astype(BF16).astype(F32)


def chunk_copies(source, target, sems):
    width = HEADS * HD // CHUNKS
    return [
        pltpu.make_async_copy(
            source.at[:, pl.ds(c * width, width)], target.at[:, pl.ds(c * width, width)], sems.at[c]
        )
        for c in range(CHUNKS)
    ]


def start_all(copies):
    for copy in copies:
        copy.start()


def wait_all(copies):
    for copy in copies:
        copy.wait()


def spread_kernel(own, far, slots):
    x = lax.axis_index("x")
    for i in range(ROW_X):

        @pl.when(i > x)
        def _():
            slots[i] = own[...]

        @pl.when(i <= x)
        def _():
            slots[i] = far[...]


def prepare_kernel(g_hbm, o_hbm, norm, ext, g, o, ext_t, g_sems, o_sems):
    copies = list(zip(chunk_copies(g_hbm, g, g_sems), chunk_copies(o_hbm, o, o_sems)))
    for pair in copies:
        start_all(pair)
    ones = jnp.ones((8, HD), BF16)
    place = lax.broadcasted_iota(jnp.int32, (8, ROWS), 0)
    for h in range(HEADS):
        if h % (HEADS // CHUNKS) == 0:
            wait_all(copies[h // (HEADS // CHUNKS)])
        product = g[:, columns(h)].astype(F32) * o[:, columns(h)].astype(F32)
        high = product.astype(BF16)
        low = (product - high.astype(F32)).astype(BF16)
        delta = dot(ones, high, NT) + dot(ones, low, NT)
        shift = jnp.broadcast_to(norm[h : h + 1, :] * (-(HD**0.5)), (8, ROWS))
        block = jnp.zeros((8, ROWS), F32)
        for r, term in enumerate(pieces(shift) + pieces(-delta)):
            block = jnp.where(place == r, term, block)
        ext_t[8 * h : 8 * h + 8, :] = block
    ext[...] = ext_t[...].T.astype(BF16)


def tile_grads(q, g, ext, k, v, bias, dq, dkv):
    lane = lax.broadcasted_iota(jnp.int32, (ROWS, HD), 1)
    k_wide = jnp.concatenate([k, jnp.where(lane % 8 < 3, 1.0, 0.0).astype(BF16)], axis=1)
    v_wide = jnp.concatenate([v, jnp.where((lane % 8 >= 3) & (lane % 8 < 6), 1.0, 0.0).astype(BF16)], axis=1)
    extras = [jnp.where(lane // 8 == h, ext[...], jnp.zeros((), BF16)) for h in range(HEADS)]
    q_wide = jnp.concatenate([jnp.concatenate([q[:, columns(h)], extras[h]], axis=1) for h in range(HEADS)], axis=0)
    g_wide = jnp.concatenate([jnp.concatenate([g[:, columns(h)], extras[h]], axis=1) for h in range(HEADS)], axis=0)
    scores = dot(q_wide, k_wide, NT)
    dprobs = dot(g_wide, v_wide, NT)
    probs = jnp.exp2(scores * (SCALE * LOG2E) + jnp.concatenate([bias[...]] * HEADS, axis=0))
    dscores = (probs * dprobs).astype(BF16)
    dq[...] += dot(dscores, k)
    q_rows = jnp.concatenate([q[:, columns(h)] for h in range(HEADS)], axis=0)
    g_rows = jnp.concatenate([g[:, columns(h)] for h in range(HEADS)], axis=0)
    dkv[:, :ROWS] = dot(q_rows, dscores, TN) * SCALE
    dkv[:, ROWS:] = dot(g_rows, probs.astype(BF16), TN)


def set_bias(bias, doc, ctx, offset):
    key_pos = (ctx - offset) * ROWS + lax.broadcasted_iota(jnp.int32, (ROWS, ROWS), 1)
    query_pos = ctx * ROWS + lax.broadcasted_iota(jnp.int32, (ROWS, ROWS), 0)
    start = jnp.broadcast_to(doc[...], (ROWS, ROWS)).T
    bias[...] = jnp.where((key_pos >= start) & (key_pos <= query_pos), 0.0, -1e30)


def near_kernel(first, doc, q, g, ext, own, far, dq_hbm, own_grads, far_grads, dq, bias, dkv, dq_sem):
    ctx = lax.axis_index(("z", "x"))
    dq[...] = jnp.zeros_like(dq)
    far_grads[...] = jnp.zeros_like(far_grads)
    set_bias(bias, doc, ctx, 0)
    tile_grads(q, g, ext, own[:ROWS], own[ROWS:], bias, dq, dkv)
    own_grads[:ROWS] = dkv[:, :ROWS].T
    own_grads[ROWS:] = dkv[:, ROWS:].T

    @pl.when(first[0] < (ctx - REACH + 1) * ROWS)
    def _():
        set_bias(bias, doc, ctx, REACH)
        tile_grads(q, g, ext, far[:ROWS], far[ROWS:], bias, dq, dkv)
        far_grads[:ROWS] = dkv[:, :ROWS].T.astype(BF16)
        far_grads[ROWS:] = dkv[:, ROWS:].T.astype(BF16)

    out = pltpu.make_async_copy(dq, dq_hbm, dq_sem)
    out.start()
    out.wait()


def between_kernel(
    first, doc, q, g, ext, blocks, near_hbm, far_grads, dq_hbm, parts, dq, near, total, bias, dkv, near_sem, dq_sems
):
    ctx, x = lax.axis_index(("z", "x")), lax.axis_index("x")
    near_copy = pltpu.make_async_copy(near_hbm, near, near_sem)
    near_copy.start()
    total[...] = jnp.zeros_like(total)
    parts[...] = jnp.zeros_like(parts)
    parts[x, : 2 * ROWS] = far_grads[...]
    reach = jnp.clip(lax.div(ctx * ROWS - first[0] + (ROWS - 1), ROWS), 0, REACH - 1)

    def one(offset, carry):
        slot = lax.rem(x - offset + ROW_X, ROW_X)
        set_bias(bias, doc, ctx, offset)
        tile_grads(q, g, ext, blocks[slot, :ROWS], blocks[slot, ROWS:], bias, total, dkv)
        parts[slot, :ROWS] = dkv[:, :ROWS].T.astype(BF16)
        parts[slot, ROWS : 2 * ROWS] = dkv[:, ROWS:].T.astype(BF16)
        return carry

    lax.fori_loop(1, reach + 1, one, 0)
    near_copy.wait()
    square = jnp.zeros((8, HD), F32)
    copies = chunk_copies(dq, dq_hbm, dq_sems)
    for h in range(HEADS):
        block = (total[rows_of(h), :] + near[rows_of(h), :]) * SCALE
        dq[:, columns(h)] = block.astype(BF16)
        square += jnp.sum((block * block).reshape(ROWS // 8, 8, HD), axis=0)
        if (h + 1) % (HEADS // CHUNKS) == 0:
            copies[h // (HEADS // CHUNKS)].start()
    square = jnp.broadcast_to(jnp.sum(square, axis=0, keepdims=True), (TAIL, HD))
    place = lax.broadcasted_iota(jnp.int32, (TAIL, HD), 0)
    rows = jnp.zeros((TAIL, HD), F32)
    for r, term in enumerate(pieces(square)):
        rows = jnp.where(place == r, term, rows)
    for i in range(ROW_X):
        parts[i, 2 * ROWS :] = rows.astype(BF16)
    wait_all(copies)


def rows_kernel(back, rows):
    row = jnp.sum(jnp.sum(back[:, 2 * ROWS :].astype(F32), axis=0), axis=0, keepdims=True)
    rows[...] = jnp.broadcast_to(row, rows.shape)


def fold_kernel(back, own_grads, rows, mine, onward):
    x = lax.axis_index("x")
    here, there = own_grads[...], jnp.zeros((2 * ROWS, HD), F32)
    for i in range(ROW_X):
        part = back[i, : 2 * ROWS].astype(F32)
        here += jnp.where(x < i, part, 0.0)
        there += jnp.where(x < i, 0.0, part)
    mine[...] = here
    onward[...] = there.astype(BF16)


def end_kernel(entries, squares, mine, arrived, grad_keys, grad_values, mean):
    grads = mine[...] + arrived[...].astype(F32)
    grad_keys[...] = grads[:ROWS].astype(BF16)
    grad_values[...] = grads[ROWS:].astype(BF16)
    mean[...] = jnp.sum(jnp.sum(squares[...], axis=0, keepdims=True), axis=1, keepdims=True) / entries


VMEM = pl.BlockSpec(memory_space=pltpu.VMEM)
SMEM = pl.BlockSpec(memory_space=pltpu.SMEM)
ANY = pl.BlockSpec(memory_space=pltpu.HBM)
DMA = pltpu.SemaphoreType.DMA


def call(kernel, ins, outs, scratch, args, limit=50, tiles=0.0):
    return pl.pallas_call(
        kernel,
        out_shape=tuple(jax.ShapeDtypeStruct(shape, dtype) for _, shape, dtype in outs),
        in_specs=ins,
        out_specs=tuple(space for space, _, _ in outs),
        scratch_shapes=[s if hasattr(s, "memory_space") or not isinstance(s, tuple) else pltpu.VMEM(*s) for s in scratch],
        compiler_params=pltpu.CompilerParams(vmem_limit_bytes=limit * 2**20),
        cost_estimate=pl.CostEstimate(
            flops=int(tiles * 10 * HEADS * ROWS * ROWS * HD), bytes_accessed=4 * 2**20, transcendentals=0
        ),
    )(*args)


def exchange_x(x):
    return lax.all_to_all(x, "x", 0, 0, tiled=True)


def shift_z(x, by):
    peers = lax.axis_size("z")
    return lax.ppermute(x, "z", [(i, (i + by) % peers) for i in range(peers)])


def shards(queries, keys, values, attn_out, grad_out, log_norm, doc_start):
    wide = ROWS * HEADS
    kv = (2 * ROWS, HD)
    full = ((ROWS, HEADS * HD), BF16)
    chunk_sems = DMA((CHUNKS,))

    place = lax.broadcasted_iota(jnp.int32, (2, ROWS, HD), 0)
    own = jnp.where(place == 0, keys[None], values[None]).reshape(kv)
    far = shift_z(own, 1)
    doc = doc_start.reshape(1, ROWS)
    (ext,) = call(
        prepare_kernel,
        [ANY, ANY, VMEM],
        [(VMEM, (ROWS, HD), BF16)],
        [full, full, ((HD, ROWS), F32), chunk_sems, chunk_sems],
        (grad_out, attn_out, log_norm),
        limit=53,
        tiles=1.0,
    )
    far, ext = lax.optimization_barrier((far, ext))
    (sent,) = call(spread_kernel, [VMEM, VMEM], [(VMEM, (ROW_X,) + kv, BF16)], [], (own, far), limit=2)
    blocks = exchange_x(sent)
    tile_scratch = [((ROWS, ROWS), F32), ((HD, 2 * ROWS), F32), DMA]
    dq_near, own_grads, far_grads = call(
        near_kernel,
        [SMEM, VMEM, VMEM, VMEM, VMEM, VMEM, VMEM],
        [(ANY, (wide, HD), F32), (VMEM, kv, F32), (VMEM, kv, BF16)],
        [((wide, HD), F32)] + tile_scratch,
        (doc_start, doc, queries, grad_out, ext, own, far),
        tiles=2.0,
    )
    blocks, dq_near, own_grads, far_grads = lax.optimization_barrier((blocks, dq_near, own_grads, far_grads))
    grad_queries, parts = call(
        between_kernel,
        [SMEM, VMEM, VMEM, VMEM, VMEM, VMEM, ANY, VMEM],
        [(ANY,) + full, (VMEM, (ROW_X, 2 * ROWS + TAIL, HD), BF16)],
        [full, ((wide, HD), F32), ((wide, HD), F32)] + tile_scratch + [chunk_sems],
        (doc_start, doc, queries, grad_out, ext, blocks, dq_near, far_grads),
        limit=50,
        tiles=3.0,
    )

    back = exchange_x(parts)
    members = ("z", "y", "core")
    (rows,) = call(rows_kernel, [VMEM], [(VMEM, (lax.axis_size(members), HD), F32)], [], (back,), limit=4)
    squares = lax.all_to_all(rows, members, 0, 0, tiled=True)
    mine, onward = call(
        fold_kernel, [VMEM, VMEM, VMEM], [(VMEM, kv, F32), (VMEM, kv, BF16)], [], (back, own_grads, rows), limit=4, tiles=5.0
    )
    arrived = shift_z(onward, -1)
    squares, mine = lax.optimization_barrier((squares, mine))
    entries = float(ROWS * HEADS * HD * lax.axis_size(("z", "x", "y", "core")))
    grad_keys, grad_values, mean = call(
        functools.partial(end_kernel, entries),
        [VMEM, VMEM, VMEM],
        [(VMEM, (ROWS, HD), BF16), (VMEM, (ROWS, HD), BF16), (VMEM, (1, 1), F32)],
        [],
        (squares, mine, arrived),
        limit=4,
    )
    return (grad_queries, grad_keys, grad_values, mean.reshape(()))


def solution(mesh):
    ctx, tp = ("z", "x"), ("y", "core")
    sizes = (mesh.shape["ctx"] // ROW_X, ROW_X, mesh.shape["tp"] // 2, 2)
    chips = Mesh(mesh.devices.reshape(sizes), ctx + tp)
    return jax.shard_map(
        shards,
        mesh=chips,
        in_specs=(P(ctx, tp), P(ctx, tp), P(ctx, tp), P(ctx, tp), P(ctx, tp), P(tp, ctx), P(ctx)),
        out_specs=(P(ctx, tp), P(ctx, tp), P(ctx, tp), P()),
        check_vma=False,
    )
```

```python
import functools
import math

import jax
import jax.numpy as jnp
from jax import lax
from jax.experimental import pallas as pl
from jax.experimental.pallas import tpu as pltpu
from jax.sharding import Mesh
from jax.sharding import PartitionSpec as P

HD = 128
ROWS = 256
HEADS = 16
REACH = 4
ROW_X = 4
LOG2E = math.log2(math.e)
SCALE = HD**-0.5
NT = (((1,), (1,)), ((), ()))
NN = (((1,), (0,)), ((), ()))
TN = (((0,), (0,)), ((), ()))
CHUNKS = 4
TAIL = 16
BF16 = jnp.bfloat16
F32 = jnp.float32


def dot(a, b, dims=NN):
    return lax.dot_general(a, b, dims, preferred_element_type=F32)


def columns(h):
    return slice(h * HD, (h + 1) * HD)


def rows_of(h):
    return slice(h * ROWS, (h + 1) * ROWS)


def pieces(x):
    first = x.astype(BF16).astype(F32)
    rest = x - first
    second = rest.astype(BF16).astype(F32)
    return first, second, (rest - second).astype(BF16).astype(F32)


def chunk_copies(source, target, sems):
    width = HEADS * HD // CHUNKS
    return [
        pltpu.make_async_copy(
            source.at[:, pl.ds(c * width, width)], target.at[:, pl.ds(c * width, width)], sems.at[c]
        )
        for c in range(CHUNKS)
    ]


def start_all(copies):
    for copy in copies:
        copy.start()


def wait_all(copies):
    for copy in copies:
        copy.wait()


def spread_kernel(own, far, slots):
    x = lax.axis_index("x")
    for i in range(ROW_X):

        @pl.when(i > x)
        def _():
            slots[i] = own[...]

        @pl.when(i <= x)
        def _():
            slots[i] = far[...]


def prepare_kernel(g_hbm, o_hbm, norm, ext, g, o, ext_t, g_sems, o_sems):
    copies = list(zip(chunk_copies(g_hbm, g, g_sems), chunk_copies(o_hbm, o, o_sems)))
    for pair in copies:
        start_all(pair)
    ones = jnp.ones((8, HD), BF16)
    place = lax.broadcasted_iota(jnp.int32, (8, ROWS), 0)
    for h in range(HEADS):
        if h % (HEADS // CHUNKS) == 0:
            wait_all(copies[h // (HEADS // CHUNKS)])
        product = g[:, columns(h)].astype(F32) * o[:, columns(h)].astype(F32)
        high = product.astype(BF16)
        low = (product - high.astype(F32)).astype(BF16)
        delta = dot(ones, high, NT) + dot(ones, low, NT)
        shift = jnp.broadcast_to(norm[h : h + 1, :] * (-(HD**0.5)), (8, ROWS))
        block = jnp.zeros((8, ROWS), F32)
        for r, term in enumerate(pieces(shift) + pieces(-delta)):
            block = jnp.where(place == r, term, block)
        ext_t[8 * h : 8 * h + 8, :] = block
    ext[...] = ext_t[...].T.astype(BF16)


def tile_grads(q, g, ext, k, v, bias, dq, dkv):
    lane = lax.broadcasted_iota(jnp.int32, (ROWS, HD), 1)
    k_wide = jnp.concatenate([k, jnp.where(lane % 8 < 3, 1.0, 0.0).astype(BF16)], axis=1)
    v_wide = jnp.concatenate([v, jnp.where((lane % 8 >= 3) & (lane % 8 < 6), 1.0, 0.0).astype(BF16)], axis=1)
    extras = [jnp.where(lane // 8 == h, ext[...], jnp.zeros((), BF16)) for h in range(HEADS)]
    q_wide = jnp.concatenate([jnp.concatenate([q[:, columns(h)], extras[h]], axis=1) for h in range(HEADS)], axis=0)
    g_wide = jnp.concatenate([jnp.concatenate([g[:, columns(h)], extras[h]], axis=1) for h in range(HEADS)], axis=0)
    scores = dot(q_wide, k_wide, NT)
    dprobs = dot(g_wide, v_wide, NT)
    probs = jnp.exp2(scores * (SCALE * LOG2E) + jnp.concatenate([bias[...]] * HEADS, axis=0))
    dscores = (probs * dprobs).astype(BF16)
    dq[...] += dot(dscores, k)
    q_rows = jnp.concatenate([q[:, columns(h)] for h in range(HEADS)], axis=0)
    g_rows = jnp.concatenate([g[:, columns(h)] for h in range(HEADS)], axis=0)
    dkv[:, :ROWS] = dot(q_rows, dscores, TN) * SCALE
    dkv[:, ROWS:] = dot(g_rows, probs.astype(BF16), TN)


def set_bias(bias, doc, ctx, offset):
    key_pos = (ctx - offset) * ROWS + lax.broadcasted_iota(jnp.int32, (ROWS, ROWS), 1)
    query_pos = ctx * ROWS + lax.broadcasted_iota(jnp.int32, (ROWS, ROWS), 0)
    start = jnp.broadcast_to(doc[...], (ROWS, ROWS)).T
    bias[...] = jnp.where((key_pos >= start) & (key_pos <= query_pos), 0.0, -1e30)


def near_kernel(first, doc, q, g, ext, own, far, dq_hbm, own_grads, far_grads, dq, bias, dkv, dq_sem):
    ctx = lax.axis_index(("z", "x"))
    dq[...] = jnp.zeros_like(dq)
    far_grads[...] = jnp.zeros_like(far_grads)
    set_bias(bias, doc, ctx, 0)
    tile_grads(q, g, ext, own[:ROWS], own[ROWS:], bias, dq, dkv)
    own_grads[:ROWS] = dkv[:, :ROWS].T
    own_grads[ROWS:] = dkv[:, ROWS:].T

    @pl.when(first[0] < (ctx - REACH + 1) * ROWS)
    def _():
        set_bias(bias, doc, ctx, REACH)
        tile_grads(q, g, ext, far[:ROWS], far[ROWS:], bias, dq, dkv)
        far_grads[:ROWS] = dkv[:, :ROWS].T.astype(BF16)
        far_grads[ROWS:] = dkv[:, ROWS:].T.astype(BF16)

    out = pltpu.make_async_copy(dq, dq_hbm, dq_sem)
    out.start()
    out.wait()


def between_kernel(
    first, doc, q, g, ext, blocks, near_hbm, far_grads, dq_hbm, parts, dq, near, total, bias, dkv, near_sem, dq_sems
):
    ctx, x = lax.axis_index(("z", "x")), lax.axis_index("x")
    near_copy = pltpu.make_async_copy(near_hbm, near, near_sem)
    near_copy.start()
    total[...] = jnp.zeros_like(total)
    parts[...] = jnp.zeros_like(parts)
    parts[x, : 2 * ROWS] = far_grads[...]
    reach = jnp.clip(lax.div(ctx * ROWS - first[0] + (ROWS - 1), ROWS), 0, REACH - 1)

    def one(offset, carry):
        slot = lax.rem(x - offset + ROW_X, ROW_X)
        set_bias(bias, doc, ctx, offset)
        tile_grads(q, g, ext, blocks[slot, :ROWS], blocks[slot, ROWS:], bias, total, dkv)
        parts[slot, :ROWS] = dkv[:, :ROWS].T.astype(BF16)
        parts[slot, ROWS : 2 * ROWS] = dkv[:, ROWS:].T.astype(BF16)
        return carry

    lax.fori_loop(1, reach + 1, one, 0)
    near_copy.wait()
    copies = chunk_copies(dq, dq_hbm, dq_sems)
    for h in range(HEADS):
        block = (total[rows_of(h), :] + near[rows_of(h), :]) * SCALE
        total[rows_of(h), :] = block
        dq[:, columns(h)] = block.astype(BF16)
        if (h + 1) % (HEADS // CHUNKS) == 0:
            copies[h // (HEADS // CHUNKS)].start()
    square = jnp.zeros((8, HD), F32)
    for h in range(HEADS):
        block = total[rows_of(h), :]
        square += jnp.sum((block * block).reshape(ROWS // 8, 8, HD), axis=0)
    square = jnp.broadcast_to(jnp.sum(square, axis=0, keepdims=True), (TAIL, HD))
    place = lax.broadcasted_iota(jnp.int32, (TAIL, HD), 0)
    rows = jnp.zeros((TAIL, HD), F32)
    for r, term in enumerate(pieces(square)):
        rows = jnp.where(place == r, term, rows)
    for i in range(ROW_X):
        parts[i, 2 * ROWS :] = rows.astype(BF16)
    wait_all(copies)


def fold_kernel(back, own_grads, rows, mine, onward):
    x = lax.axis_index("x")
    row = jnp.sum(jnp.sum(back[:, 2 * ROWS :].astype(F32), axis=0), axis=0, keepdims=True)
    rows[...] = jnp.broadcast_to(row, rows.shape)
    here, there = own_grads[...], jnp.zeros((2 * ROWS, HD), F32)
    for i in range(ROW_X):
        part = back[i, : 2 * ROWS].astype(F32)
        here += jnp.where(x < i, part, 0.0)
        there += jnp.where(x < i, 0.0, part)
    mine[...] = here
    onward[...] = there.astype(BF16)


def end_kernel(entries, squares, mine, arrived, grad_keys, grad_values, mean):
    grads = mine[...] + arrived[...].astype(F32)
    grad_keys[...] = grads[:ROWS].astype(BF16)
    grad_values[...] = grads[ROWS:].astype(BF16)
    mean[...] = jnp.sum(jnp.sum(squares[...], axis=0, keepdims=True), axis=1, keepdims=True) / entries


VMEM = pl.BlockSpec(memory_space=pltpu.VMEM)
SMEM = pl.BlockSpec(memory_space=pltpu.SMEM)
ANY = pl.BlockSpec(memory_space=pltpu.HBM)
DMA = pltpu.SemaphoreType.DMA


def call(kernel, ins, outs, scratch, args, limit=50, tiles=0.0):
    return pl.pallas_call(
        kernel,
        out_shape=tuple(jax.ShapeDtypeStruct(shape, dtype) for _, shape, dtype in outs),
        in_specs=ins,
        out_specs=tuple(space for space, _, _ in outs),
        scratch_shapes=[s if hasattr(s, "memory_space") or not isinstance(s, tuple) else pltpu.VMEM(*s) for s in scratch],
        compiler_params=pltpu.CompilerParams(vmem_limit_bytes=limit * 2**20),
        cost_estimate=pl.CostEstimate(
            flops=int(tiles * 10 * HEADS * ROWS * ROWS * HD), bytes_accessed=4 * 2**20, transcendentals=0
        ),
    )(*args)


def exchange_x(x):
    return lax.all_to_all(x, "x", 0, 0, tiled=True)


def shift_z(x, by):
    peers = lax.axis_size("z")
    return lax.ppermute(x, "z", [(i, (i + by) % peers) for i in range(peers)])


def shards(queries, keys, values, attn_out, grad_out, log_norm, doc_start):
    wide = ROWS * HEADS
    kv = (2 * ROWS, HD)
    full = ((ROWS, HEADS * HD), BF16)
    chunk_sems = DMA((CHUNKS,))

    place = lax.broadcasted_iota(jnp.int32, (2, ROWS, HD), 0)
    own = jnp.where(place == 0, keys[None], values[None]).reshape(kv)
    far = shift_z(own, 1)
    doc = doc_start.reshape(1, ROWS)
    (ext,) = call(
        prepare_kernel,
        [ANY, ANY, VMEM],
        [(VMEM, (ROWS, HD), BF16)],
        [full, full, ((HD, ROWS), F32), chunk_sems, chunk_sems],
        (grad_out, attn_out, log_norm),
        limit=53,
        tiles=1.0,
    )
    far, ext = lax.optimization_barrier((far, ext))
    (sent,) = call(spread_kernel, [VMEM, VMEM], [(VMEM, (ROW_X,) + kv, BF16)], [], (own, far), limit=2)
    blocks = exchange_x(sent)
    tile_scratch = [((ROWS, ROWS), F32), ((HD, 2 * ROWS), F32), DMA]
    dq_near, own_grads, far_grads = call(
        near_kernel,
        [SMEM, VMEM, VMEM, VMEM, VMEM, VMEM, VMEM],
        [(ANY, (wide, HD), F32), (VMEM, kv, F32), (VMEM, kv, BF16)],
        [((wide, HD), F32)] + tile_scratch,
        (doc_start, doc, queries, grad_out, ext, own, far),
        tiles=2.0,
    )
    blocks, dq_near, own_grads, far_grads = lax.optimization_barrier((blocks, dq_near, own_grads, far_grads))
    grad_queries, parts = call(
        between_kernel,
        [SMEM, VMEM, VMEM, VMEM, VMEM, VMEM, ANY, VMEM],
        [(ANY,) + full, (VMEM, (ROW_X, 2 * ROWS + TAIL, HD), BF16)],
        [full, ((wide, HD), F32), ((wide, HD), F32)] + tile_scratch + [chunk_sems],
        (doc_start, doc, queries, grad_out, ext, blocks, dq_near, far_grads),
        tiles=3.0,
    )

    back = exchange_x(parts)
    members = ("z", "y", "core")
    rows, mine, onward = call(
        fold_kernel,
        [VMEM, VMEM],
        [(VMEM, (lax.axis_size(members), HD), F32), (VMEM, kv, F32), (VMEM, kv, BF16)],
        [],
        (back, own_grads),
        limit=4,
    )
    squares = lax.all_to_all(rows, members, 0, 0, tiled=True)
    arrived = shift_z(onward, -1)
    entries = float(ROWS * HEADS * HD * lax.axis_size(("z", "x", "y", "core")))
    grad_keys, grad_values, mean = call(
        functools.partial(end_kernel, entries),
        [VMEM, VMEM, VMEM],
        [(VMEM, (ROWS, HD), BF16), (VMEM, (ROWS, HD), BF16), (VMEM, (1, 1), F32)],
        [],
        (squares, mine, arrived),
        limit=4,
    )
    return (grad_queries, grad_keys, grad_values, mean.reshape(()))


def solution(mesh):
    ctx, tp = ("z", "x"), ("y", "core")
    sizes = (mesh.shape["ctx"] // ROW_X, ROW_X, mesh.shape["tp"] // 2, 2)
    chips = Mesh(mesh.devices.reshape(sizes), ctx + tp)
    return jax.shard_map(
        shards,
        mesh=chips,
        in_specs=(P(ctx, tp), P(ctx, tp), P(ctx, tp), P(ctx, tp), P(ctx, tp), P(tp, ctx), P(ctx)),
        out_specs=(P(ctx, tp), P(ctx, tp), P(ctx, tp), P()),
        check_vma=False,
    )
```

```python
import functools
import math

import jax
import jax.numpy as jnp
from jax import lax
from jax.experimental import pallas as pl
from jax.experimental.pallas import tpu as pltpu
from jax.sharding import Mesh
from jax.sharding import PartitionSpec as P

HD = 128
ROWS = 256
HEADS = 16
REACH = 4
ROW_X = 4
LOG2E = math.log2(math.e)
SCALE = HD**-0.5
NT = (((1,), (1,)), ((), ()))
NN = (((1,), (0,)), ((), ()))
TN = (((0,), (0,)), ((), ()))
CHUNKS = 4
TAIL = 16
BF16 = jnp.bfloat16
F32 = jnp.float32


def dot(a, b, dims=NN):
    return lax.dot_general(a, b, dims, preferred_element_type=F32)


def columns(h):
    return slice(h * HD, (h + 1) * HD)


def rows_of(h):
    return slice(h * ROWS, (h + 1) * ROWS)


def pieces(x):
    first = x.astype(BF16).astype(F32)
    rest = x - first
    second = rest.astype(BF16).astype(F32)
    return first, second, (rest - second).astype(BF16).astype(F32)


def chunk_copies(source, target, sems):
    width = HEADS * HD // CHUNKS
    return [
        pltpu.make_async_copy(
            source.at[:, pl.ds(c * width, width)], target.at[:, pl.ds(c * width, width)], sems.at[c]
        )
        for c in range(CHUNKS)
    ]


def start_all(copies):
    for copy in copies:
        copy.start()


def wait_all(copies):
    for copy in copies:
        copy.wait()


def spread_kernel(own, far, slots):
    x = lax.axis_index("x")
    for i in range(ROW_X):

        @pl.when(i > x)
        def _():
            slots[i] = own[...]

        @pl.when(i <= x)
        def _():
            slots[i] = far[...]


def prepare_kernel(g_hbm, o_hbm, norm, ext, g, o, ext_t, g_sems, o_sems):
    copies = list(zip(chunk_copies(g_hbm, g, g_sems), chunk_copies(o_hbm, o, o_sems)))
    for pair in copies:
        start_all(pair)
    ones = jnp.ones((8, HD), BF16)
    place = lax.broadcasted_iota(jnp.int32, (8, ROWS), 0)
    for h in range(HEADS):
        if h % (HEADS // CHUNKS) == 0:
            wait_all(copies[h // (HEADS // CHUNKS)])
        product = g[:, columns(h)].astype(F32) * o[:, columns(h)].astype(F32)
        high = product.astype(BF16)
        low = (product - high.astype(F32)).astype(BF16)
        delta = dot(ones, high, NT) + dot(ones, low, NT)
        shift = jnp.broadcast_to(norm[h : h + 1, :] * (-(HD**0.5)), (8, ROWS))
        block = jnp.zeros((8, ROWS), F32)
        for r, term in enumerate(pieces(shift) + pieces(-delta)):
            block = jnp.where(place == r, term, block)
        ext_t[8 * h : 8 * h + 8, :] = block
    ext[...] = ext_t[...].T.astype(BF16)


def tile_grads(q, g, ext, k, v, bias, dq, dkv):
    lane = lax.broadcasted_iota(jnp.int32, (ROWS, HD), 1)
    k_wide = jnp.concatenate([k, jnp.where(lane % 8 < 3, 1.0, 0.0).astype(BF16)], axis=1)
    v_wide = jnp.concatenate([v, jnp.where((lane % 8 >= 3) & (lane % 8 < 6), 1.0, 0.0).astype(BF16)], axis=1)
    extras = [jnp.where(lane // 8 == h, ext[...], jnp.zeros((), BF16)) for h in range(HEADS)]
    q_wide = jnp.concatenate([jnp.concatenate([q[:, columns(h)], extras[h]], axis=1) for h in range(HEADS)], axis=0)
    g_wide = jnp.concatenate([jnp.concatenate([g[:, columns(h)], extras[h]], axis=1) for h in range(HEADS)], axis=0)
    scores = dot(q_wide, k_wide, NT)
    dprobs = dot(g_wide, v_wide, NT)
    probs = jnp.exp2(scores * (SCALE * LOG2E) + jnp.concatenate([bias[...]] * HEADS, axis=0))
    dscores = (probs * dprobs).astype(BF16)
    dq[...] += dot(dscores, k)
    q_rows = jnp.concatenate([q[:, columns(h)] for h in range(HEADS)], axis=0)
    g_rows = jnp.concatenate([g[:, columns(h)] for h in range(HEADS)], axis=0)
    dkv[:, :ROWS] = dot(q_rows, dscores, TN) * SCALE
    dkv[:, ROWS:] = dot(g_rows, probs.astype(BF16), TN)


def set_bias(bias, doc, ctx, offset):
    key_pos = (ctx - offset) * ROWS + lax.broadcasted_iota(jnp.int32, (ROWS, ROWS), 1)
    query_pos = ctx * ROWS + lax.broadcasted_iota(jnp.int32, (ROWS, ROWS), 0)
    start = jnp.broadcast_to(doc[...], (ROWS, ROWS)).T
    bias[...] = jnp.where((key_pos >= start) & (key_pos <= query_pos), 0.0, -1e30)


def near_kernel(first, doc, q, g, ext, own, far, dq_hbm, own_grads, far_grads, dq, bias, dkv, dq_sem):
    ctx = lax.axis_index(("z", "x"))
    dq[...] = jnp.zeros_like(dq)
    far_grads[...] = jnp.zeros_like(far_grads)
    set_bias(bias, doc, ctx, 0)
    tile_grads(q, g, ext, own[:ROWS], own[ROWS:], bias, dq, dkv)
    own_grads[:ROWS] = dkv[:, :ROWS].T
    own_grads[ROWS:] = dkv[:, ROWS:].T

    @pl.when(first[0] < (ctx - REACH + 1) * ROWS)
    def _():
        set_bias(bias, doc, ctx, REACH)
        tile_grads(q, g, ext, far[:ROWS], far[ROWS:], bias, dq, dkv)
        far_grads[:ROWS] = dkv[:, :ROWS].T.astype(BF16)
        far_grads[ROWS:] = dkv[:, ROWS:].T.astype(BF16)

    out = pltpu.make_async_copy(dq, dq_hbm, dq_sem)
    out.start()
    out.wait()


def between_kernel(
    first, doc, q, g, ext, blocks, near_hbm, far_grads, dq_hbm, parts, dq, near, total, bias, dkv, near_sem, dq_sems
):
    ctx, x = lax.axis_index(("z", "x")), lax.axis_index("x")
    near_copy = pltpu.make_async_copy(near_hbm, near, near_sem)
    near_copy.start()
    total[...] = jnp.zeros_like(total)
    parts[...] = jnp.zeros_like(parts)
    parts[x, : 2 * ROWS] = far_grads[...]
    reach = jnp.clip(lax.div(ctx * ROWS - first[0] + (ROWS - 1), ROWS), 0, REACH - 1)

    def one(offset, carry):
        slot = lax.rem(x - offset + ROW_X, ROW_X)
        set_bias(bias, doc, ctx, offset)
        tile_grads(q, g, ext, blocks[slot, :ROWS], blocks[slot, ROWS:], bias, total, dkv)
        parts[slot, :ROWS] = dkv[:, :ROWS].T.astype(BF16)
        parts[slot, ROWS : 2 * ROWS] = dkv[:, ROWS:].T.astype(BF16)
        return carry

    lax.fori_loop(1, reach + 1, one, 0)
    near_copy.wait()
    copies = chunk_copies(dq, dq_hbm, dq_sems)
    for h in range(HEADS):
        block = (total[rows_of(h), :] + near[rows_of(h), :]) * SCALE
        total[rows_of(h), :] = block
        dq[:, columns(h)] = block.astype(BF16)
        if (h + 1) % (HEADS // CHUNKS) == 0:
            copies[h // (HEADS // CHUNKS)].start()
    square = jnp.zeros((8, HD), F32)
    for h in range(HEADS):
        block = total[rows_of(h), :]
        square += jnp.sum((block * block).reshape(ROWS // 8, 8, HD), axis=0)
    square = jnp.broadcast_to(jnp.sum(square, axis=0, keepdims=True), (TAIL, HD))
    place = lax.broadcasted_iota(jnp.int32, (TAIL, HD), 0)
    rows = jnp.zeros((TAIL, HD), F32)
    for r, term in enumerate(pieces(square)):
        rows = jnp.where(place == r, term, rows)
    for i in range(ROW_X):
        parts[i, 2 * ROWS :] = rows.astype(BF16)
    wait_all(copies)


def rows_kernel(back, rows):
    row = jnp.sum(jnp.sum(back[:, 2 * ROWS :].astype(F32), axis=0), axis=0, keepdims=True)
    rows[...] = jnp.broadcast_to(row, rows.shape)


def sum_kernel(summed, rows):
    rows[...] = jnp.broadcast_to(jnp.sum(summed[...], axis=0, keepdims=True), rows.shape)


def fold_kernel(back, own_grads, rows, mine, onward):
    x = lax.axis_index("x")
    here, there = own_grads[...], jnp.zeros((2 * ROWS, HD), F32)
    for i in range(ROW_X):
        part = back[i, : 2 * ROWS].astype(F32)
        here += jnp.where(x < i, part, 0.0)
        there += jnp.where(x < i, 0.0, part)
    mine[...] = here
    onward[...] = there.astype(BF16)


def end_kernel(entries, squares, mine, arrived, grad_keys, grad_values, mean):
    grads = mine[...] + arrived[...].astype(F32)
    grad_keys[...] = grads[:ROWS].astype(BF16)
    grad_values[...] = grads[ROWS:].astype(BF16)
    mean[...] = jnp.sum(jnp.sum(squares[...], axis=0, keepdims=True), axis=1, keepdims=True) / entries


VMEM = pl.BlockSpec(memory_space=pltpu.VMEM)
SMEM = pl.BlockSpec(memory_space=pltpu.SMEM)
ANY = pl.BlockSpec(memory_space=pltpu.HBM)
DMA = pltpu.SemaphoreType.DMA


def call(kernel, ins, outs, scratch, args, limit=50, tiles=0.0):
    return pl.pallas_call(
        kernel,
        out_shape=tuple(jax.ShapeDtypeStruct(shape, dtype) for _, shape, dtype in outs),
        in_specs=ins,
        out_specs=tuple(space for space, _, _ in outs),
        scratch_shapes=[s if hasattr(s, "memory_space") or not isinstance(s, tuple) else pltpu.VMEM(*s) for s in scratch],
        compiler_params=pltpu.CompilerParams(vmem_limit_bytes=limit * 2**20),
        cost_estimate=pl.CostEstimate(
            flops=int(tiles * 10 * HEADS * ROWS * ROWS * HD), bytes_accessed=4 * 2**20, transcendentals=0
        ),
    )(*args)


def exchange_x(x):
    return lax.all_to_all(x, "x", 0, 0, tiled=True)


def shift_z(x, by):
    peers = lax.axis_size("z")
    return lax.ppermute(x, "z", [(i, (i + by) % peers) for i in range(peers)])


def shards(queries, keys, values, attn_out, grad_out, log_norm, doc_start):
    wide = ROWS * HEADS
    kv = (2 * ROWS, HD)
    full = ((ROWS, HEADS * HD), BF16)
    chunk_sems = DMA((CHUNKS,))

    place = lax.broadcasted_iota(jnp.int32, (2, ROWS, HD), 0)
    own = jnp.where(place == 0, keys[None], values[None]).reshape(kv)
    far = shift_z(own, 1)
    doc = doc_start.reshape(1, ROWS)
    (ext,) = call(
        prepare_kernel,
        [ANY, ANY, VMEM],
        [(VMEM, (ROWS, HD), BF16)],
        [full, full, ((HD, ROWS), F32), chunk_sems, chunk_sems],
        (grad_out, attn_out, log_norm),
        limit=53,
        tiles=1.0,
    )
    far, ext = lax.optimization_barrier((far, ext))
    (sent,) = call(spread_kernel, [VMEM, VMEM], [(VMEM, (ROW_X,) + kv, BF16)], [], (own, far), limit=2)
    blocks = exchange_x(sent)
    tile_scratch = [((ROWS, ROWS), F32), ((HD, 2 * ROWS), F32), DMA]
    dq_near, own_grads, far_grads = call(
        near_kernel,
        [SMEM, VMEM, VMEM, VMEM, VMEM, VMEM, VMEM],
        [(ANY, (wide, HD), F32), (VMEM, kv, F32), (VMEM, kv, BF16)],
        [((wide, HD), F32)] + tile_scratch,
        (doc_start, doc, queries, grad_out, ext, own, far),
        tiles=2.0,
    )
    blocks, dq_near, own_grads, far_grads = lax.optimization_barrier((blocks, dq_near, own_grads, far_grads))
    grad_queries, parts = call(
        between_kernel,
        [SMEM, VMEM, VMEM, VMEM, VMEM, VMEM, ANY, VMEM],
        [(ANY,) + full, (VMEM, (ROW_X, 2 * ROWS + TAIL, HD), BF16)],
        [full, ((wide, HD), F32), ((wide, HD), F32)] + tile_scratch + [chunk_sems],
        (doc_start, doc, queries, grad_out, ext, blocks, dq_near, far_grads),
        tiles=3.0,
    )

    back = exchange_x(parts)
    chip, ring = ("y", "core"), lax.axis_size("z")
    (rows,) = call(rows_kernel, [VMEM], [(VMEM, (lax.axis_size(chip), HD), F32)], [], (back,), limit=4)
    summed = lax.all_to_all(rows, chip, 0, 0, tiled=True)
    mine, onward = call(
        fold_kernel, [VMEM] * 3, [(VMEM, kv, F32), (VMEM, kv, BF16)], [], (back, own_grads, rows), limit=4, tiles=5.0
    )
    arrived = shift_z(onward, -1)
    (rows,) = call(sum_kernel, [VMEM], [(VMEM, (ring, HD), F32)], [], (summed,), limit=4, tiles=40.0)
    squares = lax.all_to_all(rows, "z", 0, 0, tiled=True)
    entries = float(ROWS * HEADS * HD * lax.axis_size(("z", "x", "y", "core")))
    grad_keys, grad_values, mean = call(
        functools.partial(end_kernel, entries),
        [VMEM, VMEM, VMEM],
        [(VMEM, (ROWS, HD), BF16), (VMEM, (ROWS, HD), BF16), (VMEM, (1, 1), F32)],
        [],
        (squares, mine, arrived),
        limit=4,
    )
    return (grad_queries, grad_keys, grad_values, mean.reshape(()))


def solution(mesh):
    ctx, tp = ("z", "x"), ("y", "core")
    sizes = (mesh.shape["ctx"] // ROW_X, ROW_X, mesh.shape["tp"] // 2, 2)
    chips = Mesh(mesh.devices.reshape(sizes), ctx + tp)
    return jax.shard_map(
        shards,
        mesh=chips,
        in_specs=(P(ctx, tp), P(ctx, tp), P(ctx, tp), P(ctx, tp), P(ctx, tp), P(tp, ctx), P(ctx)),
        out_specs=(P(ctx, tp), P(ctx, tp), P(ctx, tp), P()),
        check_vma=False,
    )
```

```python
import functools
import math

import jax
import jax.numpy as jnp
from jax import lax
from jax.experimental import pallas as pl
from jax.experimental.pallas import tpu as pltpu
from jax.sharding import Mesh
from jax.sharding import PartitionSpec as P

HD = 128
ROWS = 256
HEADS = 16
REACH = 4
ROW_X = 4
LOG2E = math.log2(math.e)
SCALE = HD**-0.5
NT = (((1,), (1,)), ((), ()))
NN = (((1,), (0,)), ((), ()))
TN = (((0,), (0,)), ((), ()))
CHUNKS = 4
TAIL = 16
BF16 = jnp.bfloat16
F32 = jnp.float32


def dot(a, b, dims=NN):
    return lax.dot_general(a, b, dims, preferred_element_type=F32)


def columns(h):
    return slice(h * HD, (h + 1) * HD)


def rows_of(h):
    return slice(h * ROWS, (h + 1) * ROWS)


def pieces(x):
    first = x.astype(BF16).astype(F32)
    rest = x - first
    second = rest.astype(BF16).astype(F32)
    return first, second, (rest - second).astype(BF16).astype(F32)


def chunk_copies(source, target, sems):
    width = HEADS * HD // CHUNKS
    return [
        pltpu.make_async_copy(
            source.at[:, pl.ds(c * width, width)], target.at[:, pl.ds(c * width, width)], sems.at[c]
        )
        for c in range(CHUNKS)
    ]


def start_all(copies):
    for copy in copies:
        copy.start()


def wait_all(copies):
    for copy in copies:
        copy.wait()


def spread_kernel(own, far, slots):
    x = lax.axis_index("x")
    for i in range(ROW_X):

        @pl.when(i > x)
        def _():
            slots[i] = own[...]

        @pl.when(i <= x)
        def _():
            slots[i] = far[...]


def prepare_kernel(g_hbm, o_hbm, norm, ext, g, o, ext_t, g_sems, o_sems):
    copies = list(zip(chunk_copies(g_hbm, g, g_sems), chunk_copies(o_hbm, o, o_sems)))
    for pair in copies:
        start_all(pair)
    ones = jnp.ones((8, HD), BF16)
    place = lax.broadcasted_iota(jnp.int32, (8, ROWS), 0)
    for h in range(HEADS):
        if h % (HEADS // CHUNKS) == 0:
            wait_all(copies[h // (HEADS // CHUNKS)])
        product = g[:, columns(h)].astype(F32) * o[:, columns(h)].astype(F32)
        high = product.astype(BF16)
        low = (product - high.astype(F32)).astype(BF16)
        delta = dot(ones, high, NT) + dot(ones, low, NT)
        shift = jnp.broadcast_to(norm[h : h + 1, :] * (-(HD**0.5)), (8, ROWS))
        block = jnp.zeros((8, ROWS), F32)
        for r, term in enumerate(pieces(shift) + pieces(-delta)):
            block = jnp.where(place == r, term, block)
        ext_t[8 * h : 8 * h + 8, :] = block
    ext[...] = ext_t[...].T.astype(BF16)


def tile_grads(q, g, ext, k, v, bias, dq, dkv, finish=None):
    lane = lax.broadcasted_iota(jnp.int32, (ROWS, HD), 1)
    k_wide = jnp.concatenate([k, jnp.where(lane % 8 < 3, 1.0, 0.0).astype(BF16)], axis=1)
    v_wide = jnp.concatenate([v, jnp.where((lane % 8 >= 3) & (lane % 8 < 6), 1.0, 0.0).astype(BF16)], axis=1)
    extras = [jnp.where(lane // 8 == h, ext[...], jnp.zeros((), BF16)) for h in range(HEADS)]
    q_wide = jnp.concatenate([jnp.concatenate([q[:, columns(h)], extras[h]], axis=1) for h in range(HEADS)], axis=0)
    g_wide = jnp.concatenate([jnp.concatenate([g[:, columns(h)], extras[h]], axis=1) for h in range(HEADS)], axis=0)
    scores = dot(q_wide, k_wide, NT)
    dprobs = dot(g_wide, v_wide, NT)
    probs = jnp.exp2(scores * (SCALE * LOG2E) + jnp.concatenate([bias[...]] * HEADS, axis=0))
    dscores = (probs * dprobs).astype(BF16)
    dq[...] += dot(dscores, k)
    if finish is not None:
        finish()
    q_rows = jnp.concatenate([q[:, columns(h)] for h in range(HEADS)], axis=0)
    g_rows = jnp.concatenate([g[:, columns(h)] for h in range(HEADS)], axis=0)
    dkv[:, :ROWS] = dot(q_rows, dscores, TN) * SCALE
    dkv[:, ROWS:] = dot(g_rows, probs.astype(BF16), TN)


def set_bias(bias, doc, ctx, offset):
    key_pos = (ctx - offset) * ROWS + lax.broadcasted_iota(jnp.int32, (ROWS, ROWS), 1)
    query_pos = ctx * ROWS + lax.broadcasted_iota(jnp.int32, (ROWS, ROWS), 0)
    start = jnp.broadcast_to(doc[...], (ROWS, ROWS)).T
    bias[...] = jnp.where((key_pos >= start) & (key_pos <= query_pos), 0.0, -1e30)


def near_kernel(first, doc, q, g, ext, own, far, dq_hbm, own_grads, far_grads, dq, bias, dkv, dq_sem):
    ctx = lax.axis_index(("z", "x"))
    dq[...] = jnp.zeros_like(dq)
    far_grads[...] = jnp.zeros_like(far_grads)
    set_bias(bias, doc, ctx, 0)
    tile_grads(q, g, ext, own[:ROWS], own[ROWS:], bias, dq, dkv)
    own_grads[:ROWS] = dkv[:, :ROWS].T
    own_grads[ROWS:] = dkv[:, ROWS:].T

    @pl.when(first[0] < (ctx - REACH + 1) * ROWS)
    def _():
        set_bias(bias, doc, ctx, REACH)
        tile_grads(q, g, ext, far[:ROWS], far[ROWS:], bias, dq, dkv)
        far_grads[:ROWS] = dkv[:, :ROWS].T.astype(BF16)
        far_grads[ROWS:] = dkv[:, ROWS:].T.astype(BF16)

    out = pltpu.make_async_copy(dq, dq_hbm, dq_sem)
    out.start()
    out.wait()


def between_kernel(
    first, doc, q, g, ext, blocks, near_hbm, far_grads, dq_hbm, parts, dq, near, total, bias, dkv, near_sem, dq_sems
):
    ctx, x = lax.axis_index(("z", "x")), lax.axis_index("x")
    near_copy = pltpu.make_async_copy(near_hbm, near, near_sem)
    near_copy.start()
    total[...] = jnp.zeros_like(total)
    parts[...] = jnp.zeros_like(parts)
    parts[x, : 2 * ROWS] = far_grads[...]
    reach = jnp.clip(lax.div(ctx * ROWS - first[0] + (ROWS - 1), ROWS), 0, REACH - 1)

    copies = chunk_copies(dq, dq_hbm, dq_sems)

    def finish():
        square = jnp.zeros((8, HD), F32)
        for h in range(HEADS):
            block = (total[rows_of(h), :] + near[rows_of(h), :]) * SCALE
            dq[:, columns(h)] = block.astype(BF16)
            square += jnp.sum((block * block).reshape(ROWS // 8, 8, HD), axis=0)
            if (h + 1) % (HEADS // CHUNKS) == 0:
                copies[h // (HEADS // CHUNKS)].start()
        square = jnp.broadcast_to(jnp.sum(square, axis=0, keepdims=True), (TAIL, HD))
        place = lax.broadcasted_iota(jnp.int32, (TAIL, HD), 0)
        rows = jnp.zeros((TAIL, HD), F32)
        for r, term in enumerate(pieces(square)):
            rows = jnp.where(place == r, term, rows)
        for i in range(ROW_X):
            parts[i, 2 * ROWS :] = rows.astype(BF16)

    def one(offset, finish):
        slot = lax.rem(x - offset + ROW_X, ROW_X)
        set_bias(bias, doc, ctx, offset)
        tile_grads(q, g, ext, blocks[slot, :ROWS], blocks[slot, ROWS:], bias, total, dkv, finish)
        parts[slot, :ROWS] = dkv[:, :ROWS].T.astype(BF16)
        parts[slot, ROWS : 2 * ROWS] = dkv[:, ROWS:].T.astype(BF16)

    def nearer(offset, carry):
        one(offset, None)
        return carry

    lax.fori_loop(1, reach, nearer, 0)
    near_copy.wait()

    @pl.when(reach > 0)
    def _():
        one(reach, finish)

    @pl.when(reach == 0)
    def _():
        finish()

    wait_all(copies)


def fold_kernel(back, own_grads, rows, mine, onward):
    x = lax.axis_index("x")
    row = jnp.sum(jnp.sum(back[:, 2 * ROWS :].astype(F32), axis=0), axis=0, keepdims=True)
    rows[...] = jnp.broadcast_to(row, rows.shape)
    here, there = own_grads[...], jnp.zeros((2 * ROWS, HD), F32)
    for i in range(ROW_X):
        part = back[i, : 2 * ROWS].astype(F32)
        here += jnp.where(x < i, part, 0.0)
        there += jnp.where(x < i, 0.0, part)
    mine[...] = here
    onward[...] = there.astype(BF16)


def end_kernel(entries, squares, mine, arrived, grad_keys, grad_values, mean):
    grads = mine[...] + arrived[...].astype(F32)
    grad_keys[...] = grads[:ROWS].astype(BF16)
    grad_values[...] = grads[ROWS:].astype(BF16)
    mean[...] = jnp.sum(jnp.sum(squares[...], axis=0, keepdims=True), axis=1, keepdims=True) / entries


VMEM = pl.BlockSpec(memory_space=pltpu.VMEM)
SMEM = pl.BlockSpec(memory_space=pltpu.SMEM)
ANY = pl.BlockSpec(memory_space=pltpu.HBM)
DMA = pltpu.SemaphoreType.DMA


def call(kernel, ins, outs, scratch, args, limit=50, tiles=0.0):
    return pl.pallas_call(
        kernel,
        out_shape=tuple(jax.ShapeDtypeStruct(shape, dtype) for _, shape, dtype in outs),
        in_specs=ins,
        out_specs=tuple(space for space, _, _ in outs),
        scratch_shapes=[s if hasattr(s, "memory_space") or not isinstance(s, tuple) else pltpu.VMEM(*s) for s in scratch],
        compiler_params=pltpu.CompilerParams(vmem_limit_bytes=limit * 2**20),
        cost_estimate=pl.CostEstimate(
            flops=int(tiles * 10 * HEADS * ROWS * ROWS * HD), bytes_accessed=4 * 2**20, transcendentals=0
        ),
    )(*args)


def exchange_x(x):
    return lax.all_to_all(x, "x", 0, 0, tiled=True)


def shift_z(x, by):
    peers = lax.axis_size("z")
    return lax.ppermute(x, "z", [(i, (i + by) % peers) for i in range(peers)])


def shards(queries, keys, values, attn_out, grad_out, log_norm, doc_start):
    wide = ROWS * HEADS
    kv = (2 * ROWS, HD)
    full = ((ROWS, HEADS * HD), BF16)
    chunk_sems = DMA((CHUNKS,))

    place = lax.broadcasted_iota(jnp.int32, (2, ROWS, HD), 0)
    own = jnp.where(place == 0, keys[None], values[None]).reshape(kv)
    far = shift_z(own, 1)
    doc = doc_start.reshape(1, ROWS)
    (ext,) = call(
        prepare_kernel,
        [ANY, ANY, VMEM],
        [(VMEM, (ROWS, HD), BF16)],
        [full, full, ((HD, ROWS), F32), chunk_sems, chunk_sems],
        (grad_out, attn_out, log_norm),
        limit=53,
        tiles=1.0,
    )
    far, ext = lax.optimization_barrier((far, ext))
    (sent,) = call(spread_kernel, [VMEM, VMEM], [(VMEM, (ROW_X,) + kv, BF16)], [], (own, far), limit=2)
    blocks = exchange_x(sent)
    tile_scratch = [((ROWS, ROWS), F32), ((HD, 2 * ROWS), F32), DMA]
    dq_near, own_grads, far_grads = call(
        near_kernel,
        [SMEM, VMEM, VMEM, VMEM, VMEM, VMEM, VMEM],
        [(ANY, (wide, HD), F32), (VMEM, kv, F32), (VMEM, kv, BF16)],
        [((wide, HD), F32)] + tile_scratch,
        (doc_start, doc, queries, grad_out, ext, own, far),
        tiles=2.0,
    )
    blocks, dq_near, own_grads, far_grads = lax.optimization_barrier((blocks, dq_near, own_grads, far_grads))
    grad_queries, parts = call(
        between_kernel,
        [SMEM, VMEM, VMEM, VMEM, VMEM, VMEM, ANY, VMEM],
        [(ANY,) + full, (VMEM, (ROW_X, 2 * ROWS + TAIL, HD), BF16)],
        [full, ((wide, HD), F32), ((wide, HD), F32)] + tile_scratch + [chunk_sems],
        (doc_start, doc, queries, grad_out, ext, blocks, dq_near, far_grads),
        tiles=3.0,
    )

    back = exchange_x(parts)
    members = ("z", "y", "core")
    rows, mine, onward = call(
        fold_kernel,
        [VMEM, VMEM],
        [(VMEM, (lax.axis_size(members), HD), F32), (VMEM, kv, F32), (VMEM, kv, BF16)],
        [],
        (back, own_grads),
        limit=4,
    )
    squares = lax.all_to_all(rows, members, 0, 0, tiled=True)
    arrived = shift_z(onward, -1)
    entries = float(ROWS * HEADS * HD * lax.axis_size(("z", "x", "y", "core")))
    grad_keys, grad_values, mean = call(
        functools.partial(end_kernel, entries),
        [VMEM, VMEM, VMEM],
        [(VMEM, (ROWS, HD), BF16), (VMEM, (ROWS, HD), BF16), (VMEM, (1, 1), F32)],
        [],
        (squares, mine, arrived),
        limit=4,
    )
    return (grad_queries, grad_keys, grad_values, mean.reshape(()))


def solution(mesh):
    ctx, tp = ("z", "x"), ("y", "core")
    sizes = (mesh.shape["ctx"] // ROW_X, ROW_X, mesh.shape["tp"] // 2, 2)
    chips = Mesh(mesh.devices.reshape(sizes), ctx + tp)
    return jax.shard_map(
        shards,
        mesh=chips,
        in_specs=(P(ctx, tp), P(ctx, tp), P(ctx, tp), P(ctx, tp), P(ctx, tp), P(tp, ctx), P(ctx)),
        out_specs=(P(ctx, tp), P(ctx, tp), P(ctx, tp), P()),
        check_vma=False,
    )
```

```python
import functools
import math

import jax
import jax.numpy as jnp
from jax import lax
from jax.experimental import pallas as pl
from jax.experimental.pallas import tpu as pltpu
from jax.sharding import Mesh
from jax.sharding import PartitionSpec as P

HD = 128
ROWS = 256
HEADS = 16
REACH = 4
ROW_X = 4
LOG2E = math.log2(math.e)
SCALE = HD**-0.5
NT = (((1,), (1,)), ((), ()))
NN = (((1,), (0,)), ((), ()))
TN = (((0,), (0,)), ((), ()))
CHUNKS = 4
TAIL = 16
BF16 = jnp.bfloat16
F32 = jnp.float32


def dot(a, b, dims=NN):
    return lax.dot_general(a, b, dims, preferred_element_type=F32)


def columns(h):
    return slice(h * HD, (h + 1) * HD)


def rows_of(h):
    return slice(h * ROWS, (h + 1) * ROWS)


def pieces(x):
    first = x.astype(BF16).astype(F32)
    rest = x - first
    second = rest.astype(BF16).astype(F32)
    return first, second, (rest - second).astype(BF16).astype(F32)


def chunk_copies(source, target, sems):
    width = HEADS * HD // CHUNKS
    return [
        pltpu.make_async_copy(
            source.at[:, pl.ds(c * width, width)], target.at[:, pl.ds(c * width, width)], sems.at[c]
        )
        for c in range(CHUNKS)
    ]


def start_all(copies):
    for copy in copies:
        copy.start()


def wait_all(copies):
    for copy in copies:
        copy.wait()


def spread_kernel(own, far, slots):
    x = lax.axis_index("x")
    for i in range(ROW_X):

        @pl.when(i > x)
        def _():
            slots[i] = own[...]

        @pl.when(i <= x)
        def _():
            slots[i] = far[...]


def prepare_kernel(g_hbm, o_hbm, norm, ext, g, o, ext_t, g_sems, o_sems):
    copies = list(zip(chunk_copies(g_hbm, g, g_sems), chunk_copies(o_hbm, o, o_sems)))
    for pair in copies:
        start_all(pair)
    ones = jnp.ones((8, HD), BF16)
    place = lax.broadcasted_iota(jnp.int32, (8, ROWS), 0)
    for h in range(HEADS):
        if h % (HEADS // CHUNKS) == 0:
            wait_all(copies[h // (HEADS // CHUNKS)])
        product = g[:, columns(h)].astype(F32) * o[:, columns(h)].astype(F32)
        high = product.astype(BF16)
        low = (product - high.astype(F32)).astype(BF16)
        delta = dot(ones, high, NT) + dot(ones, low, NT)
        shift = jnp.broadcast_to(norm[h : h + 1, :] * (-(HD**0.5)), (8, ROWS))
        block = jnp.zeros((8, ROWS), F32)
        for r, term in enumerate(pieces(shift) + pieces(-delta)):
            block = jnp.where(place == r, term, block)
        ext_t[8 * h : 8 * h + 8, :] = block
    ext[...] = ext_t[...].T.astype(BF16)


def tile_grads(q, g, ext, k, v, bias, dq, finish=None):
    lane = lax.broadcasted_iota(jnp.int32, (ROWS, HD), 1)
    k_wide = jnp.concatenate([k, jnp.where(lane % 8 < 3, 1.0, 0.0).astype(BF16)], axis=1)
    v_wide = jnp.concatenate([v, jnp.where((lane % 8 >= 3) & (lane % 8 < 6), 1.0, 0.0).astype(BF16)], axis=1)
    extras = [jnp.where(lane // 8 == h, ext[...], jnp.zeros((), BF16)) for h in range(HEADS)]
    q_wide = jnp.concatenate([jnp.concatenate([q[:, columns(h)], extras[h]], axis=1) for h in range(HEADS)], axis=0)
    g_wide = jnp.concatenate([jnp.concatenate([g[:, columns(h)], extras[h]], axis=1) for h in range(HEADS)], axis=0)
    scores = dot(q_wide, k_wide, NT)
    dprobs = dot(g_wide, v_wide, NT)
    probs = jnp.exp2(scores * (SCALE * LOG2E) + jnp.concatenate([bias[...]] * HEADS, axis=0))
    dscores = (probs * dprobs).astype(BF16)
    dq[...] += dot(dscores, k)
    if finish is not None:
        finish()
    q_rows = jnp.concatenate([q[:, columns(h)] for h in range(HEADS)], axis=0)
    g_rows = jnp.concatenate([g[:, columns(h)] for h in range(HEADS)], axis=0)
    dk = (dot(q_rows, dscores, TN) * SCALE).T
    return dk, dot(g_rows, probs.astype(BF16), TN).T


def set_bias(bias, doc, ctx, offset):
    key_pos = (ctx - offset) * ROWS + lax.broadcasted_iota(jnp.int32, (ROWS, ROWS), 1)
    query_pos = ctx * ROWS + lax.broadcasted_iota(jnp.int32, (ROWS, ROWS), 0)
    start = jnp.broadcast_to(doc[...], (ROWS, ROWS)).T
    bias[...] = jnp.where((key_pos >= start) & (key_pos <= query_pos), 0.0, -1e30)


def near_kernel(first, doc, q, g, ext, own, far, dq_hbm, own_grads, far_grads, dq, bias, dq_sem):
    ctx = lax.axis_index(("z", "x"))
    dq[...] = jnp.zeros_like(dq)
    far_grads[...] = jnp.zeros_like(far_grads)
    set_bias(bias, doc, ctx, 0)
    dk, dv = tile_grads(q, g, ext, own[:ROWS], own[ROWS:], bias, dq)
    own_grads[:ROWS] = dk
    own_grads[ROWS:] = dv

    @pl.when(first[0] < (ctx - REACH + 1) * ROWS)
    def _():
        set_bias(bias, doc, ctx, REACH)
        dk, dv = tile_grads(q, g, ext, far[:ROWS], far[ROWS:], bias, dq)
        far_grads[:ROWS] = dk.astype(BF16)
        far_grads[ROWS:] = dv.astype(BF16)

    out = pltpu.make_async_copy(dq, dq_hbm, dq_sem)
    out.start()
    out.wait()


def between_kernel(
    first, doc, q, g, ext, blocks, near_hbm, far_grads, dq_hbm, parts, dq, near, total, bias, near_sem, dq_sems
):
    ctx, x = lax.axis_index(("z", "x")), lax.axis_index("x")
    near_copy = pltpu.make_async_copy(near_hbm, near, near_sem)
    near_copy.start()
    total[...] = jnp.zeros_like(total)
    parts[...] = jnp.zeros_like(parts)
    parts[x, : 2 * ROWS] = far_grads[...]
    reach = jnp.clip(lax.div(ctx * ROWS - first[0] + (ROWS - 1), ROWS), 0, REACH - 1)

    copies = chunk_copies(dq, dq_hbm, dq_sems)

    def finish():
        square = jnp.zeros((8, HD), F32)
        for h in range(HEADS):
            block = (total[rows_of(h), :] + near[rows_of(h), :]) * SCALE
            dq[:, columns(h)] = block.astype(BF16)
            square += jnp.sum((block * block).reshape(ROWS // 8, 8, HD), axis=0)
            if (h + 1) % (HEADS // CHUNKS) == 0:
                copies[h // (HEADS // CHUNKS)].start()
        square = jnp.broadcast_to(jnp.sum(square, axis=0, keepdims=True), (TAIL, HD))
        place = lax.broadcasted_iota(jnp.int32, (TAIL, HD), 0)
        rows = jnp.zeros((TAIL, HD), F32)
        for r, term in enumerate(pieces(square)):
            rows = jnp.where(place == r, term, rows)
        for i in range(ROW_X):
            parts[i, 2 * ROWS :] = rows.astype(BF16)

    def one(offset, finish):
        slot = lax.rem(x - offset + ROW_X, ROW_X)
        set_bias(bias, doc, ctx, offset)
        dk, dv = tile_grads(q, g, ext, blocks[slot, :ROWS], blocks[slot, ROWS:], bias, total, finish)
        parts[slot, :ROWS] = dk.astype(BF16)
        parts[slot, ROWS : 2 * ROWS] = dv.astype(BF16)

    def nearer(offset, carry):
        one(offset, None)
        return carry

    lax.fori_loop(1, reach, nearer, 0)
    near_copy.wait()

    @pl.when(reach > 0)
    def _():
        one(reach, finish)

    @pl.when(reach == 0)
    def _():
        finish()

    wait_all(copies)


def fold_kernel(back, own_grads, rows, mine, onward):
    x = lax.axis_index("x")
    row = jnp.sum(jnp.sum(back[:, 2 * ROWS :].astype(F32), axis=0), axis=0, keepdims=True)
    rows[...] = jnp.broadcast_to(row, rows.shape)
    here, there = own_grads[...], jnp.zeros((2 * ROWS, HD), F32)
    for i in range(ROW_X):
        part = back[i, : 2 * ROWS].astype(F32)
        here += jnp.where(x < i, part, 0.0)
        there += jnp.where(x < i, 0.0, part)
    mine[...] = here
    onward[...] = there.astype(BF16)


def end_kernel(entries, squares, mine, arrived, grad_keys, grad_values, mean):
    grads = mine[...] + arrived[...].astype(F32)
    grad_keys[...] = grads[:ROWS].astype(BF16)
    grad_values[...] = grads[ROWS:].astype(BF16)
    mean[...] = jnp.sum(jnp.sum(squares[...], axis=0, keepdims=True), axis=1, keepdims=True) / entries


VMEM = pl.BlockSpec(memory_space=pltpu.VMEM)
SMEM = pl.BlockSpec(memory_space=pltpu.SMEM)
ANY = pl.BlockSpec(memory_space=pltpu.HBM)
DMA = pltpu.SemaphoreType.DMA


def call(kernel, ins, outs, scratch, args, limit=50, tiles=0.0):
    return pl.pallas_call(
        kernel,
        out_shape=tuple(jax.ShapeDtypeStruct(shape, dtype) for _, shape, dtype in outs),
        in_specs=ins,
        out_specs=tuple(space for space, _, _ in outs),
        scratch_shapes=[s if hasattr(s, "memory_space") or not isinstance(s, tuple) else pltpu.VMEM(*s) for s in scratch],
        compiler_params=pltpu.CompilerParams(vmem_limit_bytes=limit * 2**20),
        cost_estimate=pl.CostEstimate(
            flops=int(tiles * 10 * HEADS * ROWS * ROWS * HD), bytes_accessed=4 * 2**20, transcendentals=0
        ),
    )(*args)


def exchange_x(x):
    return lax.all_to_all(x, "x", 0, 0, tiled=True)


def shift_z(x, by):
    peers = lax.axis_size("z")
    return lax.ppermute(x, "z", [(i, (i + by) % peers) for i in range(peers)])


def shards(queries, keys, values, attn_out, grad_out, log_norm, doc_start):
    wide = ROWS * HEADS
    kv = (2 * ROWS, HD)
    full = ((ROWS, HEADS * HD), BF16)
    chunk_sems = DMA((CHUNKS,))

    place = lax.broadcasted_iota(jnp.int32, (2, ROWS, HD), 0)
    own = jnp.where(place == 0, keys[None], values[None]).reshape(kv)
    far = shift_z(own, 1)
    doc = doc_start.reshape(1, ROWS)
    (ext,) = call(
        prepare_kernel,
        [ANY, ANY, VMEM],
        [(VMEM, (ROWS, HD), BF16)],
        [full, full, ((HD, ROWS), F32), chunk_sems, chunk_sems],
        (grad_out, attn_out, log_norm),
        limit=53,
        tiles=1.0,
    )
    far, ext = lax.optimization_barrier((far, ext))
    (sent,) = call(spread_kernel, [VMEM, VMEM], [(VMEM, (ROW_X,) + kv, BF16)], [], (own, far), limit=2)
    blocks = exchange_x(sent)
    tile_scratch = [((ROWS, ROWS), F32), DMA]
    dq_near, own_grads, far_grads = call(
        near_kernel,
        [SMEM, VMEM, VMEM, VMEM, VMEM, VMEM, VMEM],
        [(ANY, (wide, HD), F32), (VMEM, kv, F32), (VMEM, kv, BF16)],
        [((wide, HD), F32)] + tile_scratch,
        (doc_start, doc, queries, grad_out, ext, own, far),
        tiles=2.0,
    )
    blocks, dq_near, own_grads, far_grads = lax.optimization_barrier((blocks, dq_near, own_grads, far_grads))
    grad_queries, parts = call(
        between_kernel,
        [SMEM, VMEM, VMEM, VMEM, VMEM, VMEM, ANY, VMEM],
        [(ANY,) + full, (VMEM, (ROW_X, 2 * ROWS + TAIL, HD), BF16)],
        [full, ((wide, HD), F32), ((wide, HD), F32)] + tile_scratch + [chunk_sems],
        (doc_start, doc, queries, grad_out, ext, blocks, dq_near, far_grads),
        tiles=3.0,
    )

    back = exchange_x(parts)
    members = ("z", "y", "core")
    rows, mine, onward = call(
        fold_kernel,
        [VMEM, VMEM],
        [(VMEM, (lax.axis_size(members), HD), F32), (VMEM, kv, F32), (VMEM, kv, BF16)],
        [],
        (back, own_grads),
        limit=4,
    )
    squares = lax.all_to_all(rows, members, 0, 0, tiled=True)
    arrived = shift_z(onward, -1)
    entries = float(ROWS * HEADS * HD * lax.axis_size(("z", "x", "y", "core")))
    grad_keys, grad_values, mean = call(
        functools.partial(end_kernel, entries),
        [VMEM, VMEM, VMEM],
        [(VMEM, (ROWS, HD), BF16), (VMEM, (ROWS, HD), BF16), (VMEM, (1, 1), F32)],
        [],
        (squares, mine, arrived),
        limit=4,
    )
    return (grad_queries, grad_keys, grad_values, mean.reshape(()))


def solution(mesh):
    ctx, tp = ("z", "x"), ("y", "core")
    sizes = (mesh.shape["ctx"] // ROW_X, ROW_X, mesh.shape["tp"] // 2, 2)
    chips = Mesh(mesh.devices.reshape(sizes), ctx + tp)
    return jax.shard_map(
        shards,
        mesh=chips,
        in_specs=(P(ctx, tp), P(ctx, tp), P(ctx, tp), P(ctx, tp), P(ctx, tp), P(tp, ctx), P(ctx)),
        out_specs=(P(ctx, tp), P(ctx, tp), P(ctx, tp), P()),
        check_vma=False,
    )
```
